256 devices in a mesh: tm: 32 (over y, z), space: 8 (over x, core).
Axes of the slice: x: 4, y: 4, z: 8, core: 2. Of those that a mesh axis runs over, the one named last changes fastest.
Arguments:
- frames: bfloat16 [960, 16, 80, 384], P('tm', 'space'), may hold values from -6 to 6
- clip_units: int32 [64], replicated, may hold values from 1 to 11, 288 in all
- out_owner: int32 [512], replicated, may hold values from 0 to 511, as said below
- w_time: bfloat16 [1152, 384], replicated, may hold values from -2 to 2
- norm_gain: float32 [384], replicated, may hold values from 0.1 to 1.9
- w_qk: bfloat16 [384, 768], replicated, may hold values from -64 to 64
- w_value: bfloat16 [384, 384], replicated, may hold values from -0.3125 to 0.3125
- w_proj: bfloat16 [384, 384], replicated, may hold values from -0.3125 to 0.3125
Outputs:
- mixed: bfloat16 [512, 16, 80, 384], P(('tm', 'space'))
The draws below stay inside these ranges and needn't reach their ends.
Inputs may be any that keep to these rules, and one draw needn't show every extreme that they name: out_owner is a permutation of the 512 slots; out_owner[o] // 16 depends only on o modulo 32.
All inputs are finite; a program needn't handle non-finite values.
Results may differ from the reference program's by a relative error of at most 0.015.
Values may be sent and summed in bfloat16 or wider, within the bound.
No kernel may reach another device: no remote copies, remote signals or barrier semaphores. Data moves between devices by JAX's collectives and lax.ppermute only.
A program may use at most 128 MiB of HBM per device.

```python
import math
import jax
import jax.numpy as jnp
import numpy as np
from jax import lax

C = 384
WID = 80
OUT_DEV = 16
CLIP_UNITS_MOST = 11
NCLIP = 64
FRAMES = 960
OUT = 512
UNITS = 288
ROWS = 16


def draw_out_owner(key, part):
    key = jax.random.fold_in(key, 11)
    first_key, second_key = jax.random.split(key)
    groups = OUT // OUT_DEV
    owners = jax.random.permutation(first_key, groups).astype(jnp.int32)
    group_keys = jax.random.split(second_key, groups)

    def one_order(group_key):
        return jax.random.permutation(group_key, OUT_DEV).astype(jnp.int32)
    places = jax.vmap(one_order)(group_keys)
    order = jnp.arange(OUT, dtype=jnp.int32)
    residue = order % groups
    quotient = order // groups
    return owners[residue] * OUT_DEV + places[residue, quotient]


def draw_w_time(key, part):
    key = jax.random.fold_in(key, 5)
    base_key, spread_key = jax.random.split(key)
    spread = jnp.exp(jax.random.uniform(spread_key, (1, C), jnp.float32, math.log(0.3), math.log(3.0)))
    base = jnp.clip(jax.random.normal(base_key, (3 * C, C), jnp.float32), -6.0, 6.0)
    return (base * spread / math.sqrt(3 * C)).astype(jnp.bfloat16)


def draw_w_qk(key, part):
    key = jax.random.fold_in(key, 9)
    base = jnp.clip(jax.random.normal(key, (C, 2 * C), jnp.float32), -6.0, 6.0)
    return (base * (1.6 / math.sqrt(C))).astype(jnp.bfloat16)


def levels(stream_key, extent, pieces, smallest, high):
    gain = 1.0
    for dim, blocks in pieces:
        draws = jax.random.uniform(jax.random.fold_in(jax.random.fold_in(stream_key, 6), dim), (blocks,), jnp.float32, smallest / len(pieces), high / len(pieces))
        gain = gain * jnp.repeat(jnp.exp(draws), extent[dim] // blocks).reshape((-1,) + (1,) * (len(extent) - 1 - dim))
    return gain


def profile(amount, total, limit, skew):
    loads = [(1 << 20) // math.isqrt(rank ** skew) + 1 for rank in range(2, amount + 1)]
    rest, given = total - limit - (amount - 1), [1] * (amount - 1)
    while rest > 0:
        movable = [i for i in range(amount - 1) if given[i] < limit]
        mass, remaining = sum([loads[i] for i in movable]), rest
        for i in movable:
            more = min(limit - given[i], max(1, remaining * loads[i] // mass), rest)
            given[i] = given[i] + more
            rest = rest - more
    return np.array([limit] + given)


def ragged_sizes(stream_key, count, total, limit, lean):
    if count == 2:
        one = jax.random.randint(stream_key, (), max(1, total - limit), min(limit, total - 1) + 1)
        return jnp.stack([one, total - one])
    sizes = jnp.asarray(profile(count, total, limit, lean), jnp.int32)
    pairs = (count - 1) // 2
    giver, sink = sizes[1:1 + 2 * pairs:2], sizes[2:2 + 2 * pairs:2]
    slack = jnp.minimum(giver - 1, limit - sink)
    moved = jax.random.randint(jax.random.fold_in(stream_key, 1), (pairs,), 0, 1 << 20) % (slack + 1)
    sizes = sizes.at[1:1 + 2 * pairs:2].set(giver - moved).at[2:2 + 2 * pairs:2].set(sink + moved)
    return sizes[jax.random.permutation(jax.random.fold_in(stream_key, 2), count)]


def normal_values(rng, shape, scale, bound, cuts=(), held_as=jnp.bfloat16):
    factor_of = levels(rng, shape, cuts, -0.22, 0.18) if cuts else 1.0
    array = jax.random.normal(rng, shape, jnp.float32) * scale * factor_of
    return jnp.minimum(jnp.maximum(array, -bound), bound).astype(held_as)


def setup_inputs(seed: int = 0) -> dict:
    keys = jax.random.split(jax.random.key(seed), 9)
    return {
        "frames": normal_values(keys[0], (FRAMES, ROWS, WID, C), 1.0, 6.0, ((0, 32), (1, 8))),
        "clip_units": ragged_sizes(keys[1], NCLIP, UNITS, CLIP_UNITS_MOST, 2).astype(jnp.int32),
        "out_owner": draw_out_owner(jax.random.fold_in(keys[8], 71), 0),
        "w_time": draw_w_time(jax.random.fold_in(keys[8], 71), 0),
        "norm_gain": jnp.clip(1.0 + 0.18 * jax.random.normal(keys[4], (C,), jnp.float32), 0.1, 1.9),
        "w_qk": draw_w_qk(jax.random.fold_in(keys[8], 71), 0),
        "w_value": normal_values(keys[6], (C, C), C ** -0.5, 0.3125),
        "w_proj": normal_values(keys[7], (C, C), C ** -0.5, 0.3125),
    }


def pick_table(table, index):
    match = index[:, None] == jnp.arange(table.shape[0], dtype=jnp.int32)[None, :]
    return lax.optimization_barrier(jnp.sum(jnp.where(match, table[None, :], 0), axis=1)).astype(jnp.int32)

def clip_layout(clip_units, total_out):
    lengths = (4 * clip_units - 3).astype(jnp.int32)
    starts = (jnp.cumsum(lengths) - lengths).astype(jnp.int32)
    counts = (2 * clip_units - 1).astype(jnp.int32)
    out_starts = (jnp.cumsum(counts) - counts).astype(jnp.int32)
    order = jnp.arange(total_out, dtype=jnp.int32)
    member = (lax.optimization_barrier(jnp.sum((out_starts[None, :] <= order[:, None]).astype(jnp.int32), axis=1)) - 1).astype(jnp.int32)
    offset = (order - pick_table(out_starts, member)).astype(jnp.int32)
    last_frame = (pick_table(starts, member) + 2 * offset).astype(jnp.int32)
    return (starts, offset, last_frame)

def frame_block(frame, norm_gain, w_qk, w_value, w_proj):
    rows_here, cols_here, channels = frame.shape
    positions = frame.reshape(rows_here * cols_here, channels)
    values32 = positions.astype(jnp.float32)
    inverse_rms = lax.rsqrt(lax.optimization_barrier(jnp.mean(values32 * values32, axis=1, keepdims=True)) + 1e-06)
    normed = (values32 * inverse_rms * norm_gain.astype(jnp.float32)[None, :]).astype(jnp.bfloat16)
    query_key = jnp.dot(normed, w_qk, preferred_element_type=jnp.float32).astype(jnp.bfloat16)
    queries = query_key[:, :channels]
    key_part = query_key[:, channels:]
    value_rows = jnp.dot(normed, w_value, preferred_element_type=jnp.float32).astype(jnp.bfloat16)
    scores = lax.dot_general(queries, key_part, (((1,), (1,)), ((), ())), preferred_element_type=jnp.float32)
    scores = scores * (1.0 / math.sqrt(channels))
    shifted = scores - lax.optimization_barrier(jnp.max(scores, axis=1, keepdims=True))
    powers = jnp.exp(shifted)
    weights = (powers / lax.optimization_barrier(jnp.sum(powers, axis=1, keepdims=True))).astype(jnp.bfloat16)
    attended = jnp.dot(weights, value_rows, preferred_element_type=jnp.float32).astype(jnp.bfloat16)
    mixed = values32 + jnp.dot(attended, w_proj, preferred_element_type=jnp.float32)
    return mixed.astype(jnp.bfloat16).reshape(frame.shape)

def reference(frames, clip_units, out_owner, w_time, norm_gain, w_qk, w_value, w_proj):
    total_out = out_owner.shape[0]
    channels = w_value.shape[0]
    starts, offset, last_frame = clip_layout(clip_units, total_out)
    source = jnp.zeros((total_out,), jnp.int32).at[out_owner].set(jnp.arange(total_out, dtype=jnp.int32))

    def one_slot(slot):
        output = source[slot]
        newest = last_frame[output]
        early = (offset[output] >= 1).astype(frames.dtype)
        oldest = lax.dynamic_index_in_dim(frames, jnp.maximum(newest - 2, 0).astype(jnp.int32), 0, keepdims=False)
        middle = lax.dynamic_index_in_dim(frames, jnp.maximum(newest - 1, 0).astype(jnp.int32), 0, keepdims=False)
        latest = lax.dynamic_index_in_dim(frames, newest.astype(jnp.int32), 0, keepdims=False)
        stacked = jnp.concatenate([oldest * early, middle * early, latest], axis=-1)
        down = jnp.dot(stacked.reshape(-1, 3 * channels), w_time, preferred_element_type=jnp.float32)
        down = down.astype(jnp.bfloat16).reshape(latest.shape)
        return frame_block(down, norm_gain, w_qk, w_value, w_proj)
    return lax.map(one_slot, jnp.arange(total_out, dtype=jnp.int32))
```

```python
from functools import partial
import math

import jax
import jax.numpy as jnp
from jax import lax
from jax.experimental import pallas as pl
from jax.experimental.pallas import tpu as pltpu
from jax.sharding import PartitionSpec as P

SHARES = (5, 5)
GROUP = 9
COPIES = 5
NY, NZ = 4, 8
SWAP = 13
MERGED = (8, 6, 6, 6)
YCAP = 5
MIB = 1024 * 1024


def conv_kernel(slots_row, first, plan_ref, frames_ref, halo_ref, w_ref, *refs):
    *out_refs, weights, held, lhs, sems = refs
    rows, channels = held.shape[-2:]
    band = pl.ds(first, rows)
    halo, frames = halo_ref.shape[0], frames_ref.shape[0]
    per_copy = frames // COPIES
    copies = [
        pltpu.make_async_copy(
            frames_ref.at[pl.ds(i * per_copy, per_copy), band],
            held.at[pl.ds(halo + i * per_copy, per_copy)],
            sems.at[i],
        )
        for i in range(COPIES)
    ]
    copies.append(pltpu.make_async_copy(halo_ref.at[:, band], held.at[pl.ds(0, halo)], sems.at[COPIES]))
    copies.append(pltpu.make_async_copy(w_ref, weights, sems.at[COPIES + 1]))
    for copy in copies:
        copy.start()
    for copy in copies:
        copy.wait()
    count = plan_ref[ROWS_OF["own"], 0]

    def one_group(group, carry):
        for k in range(GROUP):
            slot = jnp.minimum(group * GROUP + k, count - 1)
            last = plan_ref[ROWS_OF["last"], slot]
            early = plan_ref[ROWS_OF["early"], slot] == 1
            here = pl.ds(k * rows, rows)
            lhs[here, 2 * channels :] = held[last + 2]
            for tap in range(2):
                there = pl.ds(tap * channels, channels)

                @pl.when(early)
                def _():
                    lhs[here, there] = held[last + tap]

                @pl.when(jnp.logical_not(early))
                def _():
                    lhs[here, there] = jnp.zeros((rows, channels), lhs.dtype)
        down = jnp.dot(lhs[...], weights[...], preferred_element_type=jnp.float32)
        for k in range(GROUP):
            slot = jnp.minimum(group * GROUP + k, count - 1)
            target, begin = plan_ref[slots_row, slot], 0
            piece = down[k * rows : (k + 1) * rows].astype(held.dtype)
            for out_ref in out_refs:
                slots = out_ref.shape[0]

                @pl.when((target >= begin) & (target < begin + slots))
                def _():
                    out_ref[jnp.clip(target - begin, 0, slots - 1)] = piece

                begin += slots
        return carry

    lax.fori_loop(0, lax.div(count + GROUP - 1, GROUP), one_group, 0)


def conv(plan, slots_row, frames, halo, w_time, first, rows, outs):
    count, band, channels = frames.shape
    return pl.pallas_call(
        partial(conv_kernel, slots_row, first),
        grid=(1,),
        out_shape=[jax.ShapeDtypeStruct((slots, rows, channels), frames.dtype) for slots in outs],
        in_specs=[
            pl.BlockSpec(memory_space=pltpu.SMEM),
            pl.BlockSpec(memory_space=pltpu.HBM),
            pl.BlockSpec(memory_space=pltpu.HBM),
            pl.BlockSpec(memory_space=pltpu.HBM),
        ],
        out_specs=[pl.BlockSpec((slots, rows, channels), lambda i: (0, 0, 0)) for slots in outs],
        scratch_shapes=[
            pltpu.VMEM(w_time.shape, w_time.dtype),
            pltpu.VMEM((count + 2, rows, channels), frames.dtype),
            pltpu.VMEM((GROUP * rows, 3 * channels), frames.dtype),
            pltpu.SemaphoreType.DMA((COPIES + 2,)),
        ],
        compiler_params=pltpu.CompilerParams(vmem_limit_bytes=24 * MIB),
        cost_estimate=pl.CostEstimate(
            flops=count * rows * 3 * channels * channels,
            bytes_accessed=4 * (count + sum(outs)) * rows * channels,
            transcendentals=0,
        ),
        name="temporal_conv",
    )(plan, frames, halo, w_time)


def place_kernel(row, sizes, outs, plan_ref, *refs):
    out_refs = refs[len(refs) - len(outs) :]
    at = 0
    for ref, size in zip(refs, sizes):

        def one_slot(j, carry, ref=ref, at=at):
            slot = plan_ref[row, at + j]
            begin = 0
            for out_ref, slots in zip(out_refs, outs):

                @pl.when((slot >= begin) & (slot < begin + slots))
                def _():
                    out_ref[jnp.clip(slot - begin, 0, slots - 1)] = ref[j]

                begin += slots
            return carry

        lax.fori_loop(0, size, one_slot, 0, unroll=True)
        at += size


def place(plan, row, outs, *sources, after=()):
    rows, channels = sources[0][0].shape[1:]
    sizes = [size for _, size in sources]
    results = pl.pallas_call(
        partial(place_kernel, row, sizes, outs),
        grid=(1,),
        out_shape=[jax.ShapeDtypeStruct((slots, rows, channels), sources[0][0].dtype) for slots in outs],
        in_specs=[pl.BlockSpec(memory_space=pltpu.SMEM)]
        + [pl.BlockSpec((size, rows, channels), lambda i: (0, 0, 0)) for size in sizes]
        + [pl.BlockSpec(memory_space=pl.ANY)] * len(after),
        out_specs=[pl.BlockSpec((slots, rows, channels), lambda i: (0, 0, 0)) for slots in outs],
        compiler_params=pltpu.CompilerParams(vmem_limit_bytes=16 * MIB),
        cost_estimate=pl.CostEstimate(flops=0, bytes_accessed=sum(outs), transcendentals=0),
        name="place_slots",
    )(plan, *[array for array, _ in sources], *after)
    return results if len(outs) > 1 else results[0]


ROWS_OF = {"own": 0, "last": 1, "early": 2, "ring": 3, "direct_out": 4, "collect": 5, "direct_in": 6, "merge": 7, "columns": 8, "collect_near": 9}
PLAN_ROWS = 16
LANES = 128


def plan_kernel(fr_dev, n_space, place_ref, units_ref, owner_ref, out_ref):
    n_clips = units_ref.shape[1]
    out_dev, n_time = owner_ref.shape
    bits = n_time.bit_length() - 1
    out_bits = out_dev.bit_length() - 1
    time = place_ref[0]
    y, z = lax.shift_right_logical(time, 3), time & (NZ - 1)
    up = (z + place_ref[1]) & 1
    sign = 2 * up - 1

    def sub(rows, columns):
        return lax.broadcasted_iota(jnp.int32, (rows, columns), 0)

    def lane(rows, columns):
        return lax.broadcasted_iota(jnp.int32, (rows, columns), 1)

    def total(mask, value, axis):
        picked = jnp.where(mask, value, 0).astype(jnp.float32)
        return jnp.sum(picked, axis=axis, keepdims=True).astype(jnp.int32)

    def flip(row):
        n = row.shape[1]
        return total(sub(n, n) == lane(n, n), row, 1)

    units = units_ref[...]
    lengths, counts = 4 * units - 3, 2 * units - 1
    square = (n_clips, n_clips)
    lengths_col, counts_col = flip(lengths), flip(counts)
    starts = total(sub(*square) < lane(*square), lengths_col, 0)
    starts_col = total(lane(*square) < sub(*square), lengths, 1)
    first_col = lax.shift_right_logical(starts_col + sub(n_clips, 1), 1)

    def before(edges):
        return jnp.clip(lax.shift_right_arithmetic(edges - starts + 1, 1), 0, counts)

    low_col = total(True, before(fr_dev * sub(n_time, n_clips)), 1)
    high_col = total(True, before(fr_dev * sub(n_time, n_clips) + fr_dev), 1)
    ts, tl = sub(n_time, n_time), lane(n_time, n_time)
    low = total(ts == tl, low_col, 0)
    high = total(ts == tl, high_col, 0)
    owners = lax.shift_right_logical(owner_ref[0:1, :], out_bits)
    owners_col = flip(owners)
    residue = total(owners_col == tl, ts, 0)
    residue_col = total(owners == ts, tl, 1)

    def put(name, row):
        out_ref[ROWS_OF[name] : ROWS_OF[name] + 1, 0 : row.shape[1]] = row

    def in_window(residues, lows, highs):
        return ((residues - lows) & (n_time - 1)) < highs - lows

    my_low = total(tl[0:1] == time, low, 1)
    my_high = total(tl[0:1] == time, high, 1)
    outs = my_low + tl[0:1]
    first_last = first_col + counts_col
    inside = (first_col <= outs) & (outs < first_last)
    lasts = total(inside, starts_col - 2 * first_col, 0) + 2 * outs - time * fr_dev
    put("last", lasts)
    put("early", total(inside & (outs > first_col), 1, 0))
    dests = total(ts == (outs & (n_time - 1)), owners_col, 0)
    put("direct_out", dests)
    mine = in_window(residue_col, my_low, my_high)

    def apart_of(device):
        return (sign * ((device & (NZ - 1)) - z)) & (NZ - 1)

    def key_of(device):
        return apart_of(device) * NY + lax.shift_right_logical(device, 3)

    far, far_d = apart_of(ts) >= 4, apart_of(dests) >= 4
    lower = mine & (key_of(ts) < key_of(dests)) & ((far & far_d) | (apart_of(ts) == apart_of(dests)))
    put("ring", jnp.where(far_d, 4 * NY, NY * apart_of(dests)) + total(lower, 1, 0))

    spot = lane(1, LANES)
    partner = y * NZ + ((z - sign) & (NZ - 1))
    mate_low = total(tl[0:1] == partner, low, 1)
    mate_high = total(tl[0:1] == partner, high, 1)
    mate = in_window(residue_col, mate_low, mate_high) & (apart_of(ts[:, 0:1]) < 4)
    mate_row = total(ts == tl, mate.astype(jnp.int32), 0)
    mine_row = total(ts == tl, mine.astype(jnp.int32), 0)
    mate_key_s, mate_key_l = (7 - apart_of(ts)) * NY + lax.shift_right_logical(ts, 3), (
        7 - apart_of(tl)
    ) * NY + lax.shift_right_logical(tl, 3)
    sent_at = total(mate_key_l < mate_key_s, mate_row, 1)
    same_column = (ts & (NZ - 1)) == (tl & (NZ - 1))
    merged_at = total(same_column, mine_row, 1) + total(same_column & (tl < ts), mate_row, 1)
    start_of = [sum(MERGED[:i]) for i in range(4)]
    none = sum(MERGED)

    def start_at(apart):
        return jnp.where(apart == 0, start_of[0], start_of[1] + MERGED[1] * (apart - 1))

    merged_at = merged_at + start_at(apart_of(ts[:, 0:1]))
    from_mate = total(mate & (sent_at == lane(n_time, LANES) - 4 * NY), merged_at - none, 0)
    wide = lane(n_time, LANES)
    own_count = total(mine & (apart_of(sub(n_time, LANES)) == lax.shift_right_logical(wide, 2)), 1, 0)
    rank = spot & (NY - 1)
    from_own = jnp.where(rank < own_count, start_at(lax.shift_right_logical(spot, 2)) + rank - none, 0)
    put("merge", none + jnp.where(spot < 4 * NY, from_own, from_mate))

    each = sub(n_time, n_time)
    other = lane(n_time, n_time)

    def parts_of(e):
        return lax.shift_right_logical(e, 2), e & (NY - 1)

    apart, k = parts_of(each)
    apart_o, k_o = parts_of(other)
    e_low = total(tl == y * NZ + ((z + sign * apart) & (NZ - 1)), low, 1)
    e_high = total(tl == y * NZ + ((z + sign * apart) & (NZ - 1)), high, 1)
    e_residue = total(tl == NZ * k + z, residue, 1)
    held = in_window(e_residue, e_low, e_high)
    held_row = total(ts == tl, held.astype(jnp.int32), 0)
    sooner = ((z + sign * apart_o) & (NZ - 1)) < ((z + sign * apart) & (NZ - 1))
    y_rank = total((k_o == k) & sooner, held_row, 1)
    y_slot = ((k[:, 0:1] - y) & (NY - 1)) * YCAP + y_rank
    none = NY * YCAP

    def list_of(a):
        return jnp.where((a == 0) | (a == 7), 0, jnp.where(a <= 2, 1, jnp.where(a <= 4, 3, 2)))

    def order_of(a, k):
        second = (a == 7) | (a == 2) | (a == 5) | (a == 4)
        return jnp.where(second, NY, 0) + k

    which = list_of(apart)
    earlier = (which == list_of(apart_o)) & (order_of(apart_o, k_o) < order_of(apart, k))
    listed = which[:, 0:1]
    listed = jnp.where(listed == 0, 0, MERGED[0] + MERGED[1] * (3 - listed))
    position = listed + total(earlier, held_row, 1)
    hit = held & (position == lane(n_time, LANES))
    put("columns", none + total(hit, y_slot - none, 0))

    my_residue = total(tl[0:1] == time, residue, 1)
    each_dev = out_dev // n_space
    my_outs = my_residue + n_time * sub(out_dev, 1)
    places = total(lane(out_dev, n_time) == my_residue, owner_ref[...], 1) & (out_dev - 1)
    space = place_ref[1]
    to_space = lax.shift_right_logical(places, each_dev.bit_length() - 1)
    ahead = lax.shift_right_logical(to_space, 1) - lax.shift_right_logical(space, 1)
    ahead = ahead & (n_space // 2 - 1)
    crossed = (to_space & 1) ^ (space & 1)
    near = (2 * ahead + crossed) * each_dev + (places & (each_dev - 1))
    y_from = jnp.zeros((out_dev, 1), jnp.int32)
    below = jnp.zeros((out_dev, 1), jnp.int32)
    for number in range(1, NY):
        edge = low[:, NZ * number : NZ * number + 1]
        past = my_outs >= edge
        y_from = y_from + past.astype(jnp.int32)
        under = jnp.maximum(0, lax.shift_right_arithmetic(edge - my_residue + n_time - 1, bits))
        below = jnp.where(past, under, below)
    far_first = (y - y_from) & (NY - 1)
    far_first = jnp.where(far_first == 1, 2, jnp.where(far_first == 2, 1, far_first))
    slot = far_first * YCAP + sub(out_dev, 1) - below
    put("collect", out_dev + total(slot == lane(out_dev, LANES), places - out_dev, 0))
    put("collect_near", out_dev + total(slot == lane(out_dev, LANES), near - out_dev, 0))
    t_from = total(my_outs >= high, 1, 1)
    put("direct_in", out_dev + total(t_from == lane(out_dev, LANES), places - out_dev, 0))

    everywhere = in_window(residue, low_col, high_col).astype(jnp.float32)
    same_ring = lax.shift_right_logical(ts, 3) == lax.shift_right_logical(tl, 3)

    def gathered(mask, right):
        return jnp.dot(mask.astype(jnp.float32), right, preferred_element_type=jnp.float32)

    arriving = gathered(same_ring, everywhere)
    worst = jnp.max(arriving - YCAP, axis=1, keepdims=True)
    alike = (ts & (NZ - 1)) == (tl & (NZ - 1))
    pairs = jnp.dot(everywhere, alike.astype(jnp.float32), preferred_element_type=jnp.float32)
    for way in (1, -1):
        ahead = (way * (tl - ts)) & (NZ - 1)
        behind = (way * (ts - tl)) & (NZ - 1)
        swapped = jnp.sum(jnp.where(ahead >= 4, everywhere, 0.0), axis=1, keepdims=True)
        worst = jnp.maximum(worst, swapped - SWAP)
        sums = gathered(same_ring & (behind < 2), pairs)
        over = jnp.where((ahead >= 1) & (ahead <= 3), sums, 0.0) - MERGED[1]
        worst = jnp.maximum(worst, jnp.max(over, axis=1, keepdims=True))
    worst = jnp.max(worst, axis=0, keepdims=True).astype(jnp.int32)
    put("own", jnp.where(spot == 0, my_high - my_low, worst))


def make_plan(clip_units, out_owner, here, fr_dev, n_space):
    n_time = NY * NZ
    vmem = pl.BlockSpec(memory_space=pltpu.VMEM)
    return pl.pallas_call(
        partial(plan_kernel, fr_dev, n_space),
        out_shape=jax.ShapeDtypeStruct((PLAN_ROWS, LANES), jnp.int32),
        in_specs=[pl.BlockSpec(memory_space=pltpu.SMEM), vmem, vmem],
        out_specs=vmem,
        compiler_params=pltpu.CompilerParams(vmem_limit_bytes=8 * MIB),
        name="routing_plan",
    )(here, clip_units.reshape(1, -1), out_owner.reshape(-1, n_time))


def ring_perm(dy):
    return [
        (a * NZ + b, (a + dy) % NY * NZ + b) for a in range(NY) for b in range(NZ)
    ]


def signed_perm(n_space, apart):
    moves = []
    for time in range(NY * NZ):
        for space in range(n_space):
            z = time % NZ
            sign = 1 if (z + space) % 2 else -1
            to = time - z + (z + sign * apart) % NZ
            moves.append((time * n_space + space, to * n_space + space))
    return moves


def swap_space(placed, n_space):
    each, rows, channels = placed.shape[0] // n_space, *placed.shape[1:]
    placed = placed.reshape(n_space, each, rows, channels)
    return lax.all_to_all(placed, "space", split_axis=0, concat_axis=0, tiled=True)


def far_first(n_space):
    half = n_space // 2
    return sorted(range(n_space), key=lambda o: (o != 0, -min(o // 2, half - o // 2), o))


def to_space(placed, n_space):
    each, half = placed.shape[0] // n_space, n_space // 2
    arrived = [placed]
    for offset in far_first(n_space)[1:]:
        ahead, cross = offset // 2, offset % 2
        moves = [(x * 2 + c, (x + ahead) % half * 2 + (c ^ cross)) for x in range(half) for c in range(2)]
        arrived.append(lax.ppermute(placed[each * offset : each * (offset + 1)], "space", moves))
    return arrived


def by_rings(plan, own, out_dev, n_space):
    both = ("tm", "space")
    chunks = range(len(own))
    swapped = [lax.ppermute(far, both, signed_perm(n_space, -1)) for _, far in own]
    merged = [
        place(
            plan,
            ROWS_OF["merge"],
            MERGED,
            (own[c][0], 4 * NY),
            (swapped[c], SWAP),
        )
        for c in chunks
    ]
    arrived = []
    for c in chunks:
        moved = {
            apart: lax.ppermute(merged[c][apart], both, signed_perm(n_space, apart)) for apart in (3, 2, 1)
        }
        arrived.append([merged[c][0]] + [moved[apart] for apart in (3, 2, 1)])
    columns = []
    for c in chunks:
        sources = zip(arrived[c], MERGED)
        ahead = merged[c + 1][:1] if c + 1 < len(own) else []
        columns.append(place(plan, ROWS_OF["columns"], (YCAP,) * NY, *sources, after=ahead))
    parts = []
    for c in chunks:
        last = c + 1 == len(own)
        moved = [columns[c][0]] + [lax.ppermute(columns[c][dy], "tm", ring_perm(dy)) for dy in (2, 1, 3)]
        table = "collect_near" if last else "collect"
        ahead = [] if last else columns[c + 1][:1]
        placed = place(plan, ROWS_OF[table], (out_dev,), *[(m, YCAP) for m in moved], after=ahead)
        parts.append(placed if last else swap_space(placed, n_space))
    return parts


def per_device(frames, clip_units, out_owner, w_time, norm_gain, w_qk, w_value, w_proj):
    n_time = lax.axis_size("tm")
    n_space = lax.axis_size("space")
    fr_dev, rows_dev, columns, channels = frames.shape
    out_dev = out_owner.shape[0] // n_time
    band = rows_dev * columns
    pieces = band // 16
    edges = [round(pieces * sum(SHARES[:i]) / sum(SHARES)) * 16 for i in range(len(SHARES) + 1)]
    rows_of = list(zip(edges[:-1], [b - a for a, b in zip(edges[:-1], edges[1:])]))
    time = lax.axis_index("tm").astype(jnp.int32)
    frames = frames.reshape(fr_dev, band, channels)
    halo = lax.ppermute(frames[fr_dev - 2 :], "tm", [(i, i + 1) for i in range(n_time - 1)])
    here = jnp.stack([time, lax.axis_index("space").astype(jnp.int32)])
    plan = make_plan(clip_units, out_owner, here, fr_dev, n_space)
    fits = plan[ROWS_OF["own"], 1] <= 0
    def rings():
        own = [conv(plan, ROWS_OF["ring"], frames, halo, w_time, *r, (4 * NY, SWAP)) for r in rows_of]
        return by_rings(plan, own, out_dev, n_space)

    def direct():
        send = conv(plan, ROWS_OF["direct_out"], frames, halo, w_time, 0, band, (n_time,))[0]
        received = lax.all_to_all(send, "tm", split_axis=0, concat_axis=0, tiled=True)
        placed = place(plan, ROWS_OF["direct_in"], (out_dev,), (received, n_time))
        parts = [swap_space(placed[:, first : first + rows], n_space) for first, rows in rows_of[:-1]]
        each = out_dev // n_space
        shift = lax.axis_index("space")
        first, rows = rows_of[-1]
        ends = placed[:, first : first + rows]
        near = []
        for offset in range(n_space):
            to = 2 * ((shift // 2 + offset // 2) % (n_space // 2)) + (shift + offset) % 2
            near.append(lax.dynamic_slice_in_dim(ends, each * to, each))
        return parts + [jnp.concatenate(near)]

    parts = lax.cond(fits, rings, direct)
    parts = parts[:-1] + [to_space(parts[-1], n_space)]
    w_scores = lax.dot_general(
        w_qk[:, :channels], w_qk[:, channels:], (((1,), (1,)), ((), ())), preferred_element_type=jnp.float32
    )
    w_scores = (w_scores * (math.log2(math.e) / math.sqrt(channels))).astype(frames.dtype)
    w_mix = jnp.dot(w_value, w_proj, preferred_element_type=jnp.float32).astype(frames.dtype)
    mixed = attend(here, parts, norm_gain[None, :], w_scores, w_mix)
    return mixed.reshape(out_dev // n_space, n_space * rows_dev, columns, channels)


def attend_kernel(n_space, sizes, here_ref, *refs):
    swapped = len(sizes) - 1
    gain_ref, score_ref, mix_ref, out_ref, normed, queries, values = refs[swapped + n_space :]
    space = here_ref[1]
    x, core = lax.shift_right_logical(space, 1), space & 1
    pieces = []
    at = 0
    for c, rows in enumerate(sizes):
        for i, offset in enumerate(far_first(n_space)):
            part = refs[c].at[i] if c < swapped else refs[swapped + i]
            down = part[...].astype(jnp.float32)
            inverse = lax.rsqrt(jnp.mean(down * down, axis=1, keepdims=True) + 1e-06)
            normed[at : at + rows, :] = (down * inverse * gain_ref[...]).astype(normed.dtype)
            source = ((x - offset // 2) & (n_space // 2 - 1)) * 2 + (core ^ (offset % 2))
            pieces.append((part, at, rows, i if c < swapped else source, sum(sizes[:c])))
            at += rows
    queries[...] = jnp.dot(normed[...], score_ref[...], preferred_element_type=jnp.float32).astype(queries.dtype)
    values[...] = jnp.dot(normed[...], mix_ref[...], preferred_element_type=jnp.float32).astype(values.dtype)
    per_block = n_space
    for b in range(0, len(pieces), per_block):
        block = pieces[b : b + per_block]
        begin, end = block[0][1], block[-1][1] + block[-1][2]
        scores = lax.dot_general(
            queries[begin:end, :], normed[...], (((1,), (1,)), ((), ())), preferred_element_type=jnp.float32
        )
        powers = jnp.exp2(scores - jnp.max(scores, axis=1, keepdims=True))
        sums = jnp.sum(powers, axis=1, keepdims=True)
        mixed = jnp.dot(powers.astype(values.dtype), values[...], preferred_element_type=jnp.float32)
        mixed = mixed / sums
        for part, at, rows, source, first in block:
            result = part[...].astype(jnp.float32) + mixed[at - begin : at - begin + rows]
            out_ref[source, first : first + rows] = result.astype(out_ref.dtype)


def attend(here, parts, norm_gain, w_scores, w_mix):
    *swapped, near = parts
    n_space = len(near)
    sizes = [part.shape[2] for part in swapped] + [near[0].shape[1]]
    frames, last, channels = near[-1].shape
    band = sum(sizes)
    total = n_space * band
    return pl.pallas_call(
        partial(attend_kernel, n_space, sizes),
        grid=(frames,),
        out_shape=jax.ShapeDtypeStruct((frames, n_space, band, channels), near[0].dtype),
        in_specs=[pl.BlockSpec(memory_space=pltpu.SMEM)]
        + [pl.BlockSpec((n_space, None, rows, channels), lambda i: (0, i, 0, 0)) for rows in sizes[:-1]]
        + [pl.BlockSpec((None, last, channels), lambda i: (i, 0, 0))] * n_space
        + [
            pl.BlockSpec((1, channels), lambda i: (0, 0)),
            pl.BlockSpec((channels, channels), lambda i: (0, 0)),
            pl.BlockSpec((channels, channels), lambda i: (0, 0)),
        ],
        out_specs=pl.BlockSpec((None, n_space, band, channels), lambda i: (i, 0, 0, 0)),
        scratch_shapes=[pltpu.VMEM((total, channels), near[0].dtype)] * 3,
        compiler_params=pltpu.CompilerParams(vmem_limit_bytes=32 * MIB),
        cost_estimate=pl.CostEstimate(
            flops=frames * total * (4 * channels * channels + 4 * total * channels),
            bytes_accessed=4 * frames * total * channels,
            transcendentals=frames * total * total,
        ),
        name="frame_attention",
    )(here, *swapped, *near, norm_gain, w_scores, w_mix)


def solution(mesh):
    placed = (P("tm", "space", None, None), P(), P(), P(), P(), P(), P(), P())
    return jax.shard_map(
        per_device,
        mesh=mesh,
        in_specs=placed,
        out_specs=P(("tm", "space"), None, None, None),
        check_vma=False,
    )
```
